32 devices in a mesh: parts: 2 (over x), gx: 8 (over z, y), gy: 2 (over core).
Axes of the slice: x: 2, y: 2, z: 4, core: 2. Of those that a mesh axis runs over, the one named last changes fastest.
Arguments:
- volume: float32 [4, 256, 4096], P(None, ('parts', 'gx'), 'gy'), parts along dimension 1, may hold values from -280 to 280
- mask: int32 [4, 256, 4096], P(None, ('parts', 'gx'), 'gy'), parts along dimension 1, may hold values from 0 to 1, as said below
- res_index: int32 [4], P('parts'), parts along dimension 0, may hold values from 0 to 7
Outputs:
- fine_statistic: float32 [4, 256, 4096], P(None, ('parts', 'gx'), 'gy'), parts along dimension 1
- coarse_statistic: float32 [4, 256, 4096], P(None, ('parts', 'gx'), 'gy'), parts along dimension 1
The draws below stay inside these ranges and needn't reach their ends.
There are 2 independent parts, one for each index of `parts`. The reference program is written for one: setup_inputs(seed, part) draws one part's arguments, and reference() takes and returns one part's arrays. A program takes and returns all parts, laid end to end along the dimension named above; each array names one. Nothing has to cross between parts.
Inputs may be any that keep to these rules, and one draw needn't show every extreme that they name: `mask`: 1 marks a background voxel; every 16th voxel of the first plane along both grid dimensions is background.
All inputs are finite; a program needn't handle non-finite values.
Results may differ from the reference program's by a relative error of at most 0.000054.
Values sent between devices are 32-bit elements; how exact they have to be, the bound alone decides.
A program may use at most 64 MiB of HBM per device.

```python
import math
import jax
import jax.numpy as jnp
from jax import lax

PLANES = 4
CX = 16
CY = 2048
HALO = 8
ZREACH = 2
NX = 128
NY = 4096


def draw_volume(key, part):
    key = jax.random.fold_in(key, 11)
    first, second, third, fourth = jax.random.split(key, 4)
    cube_shape = (PLANES, NX, NY)
    base = jnp.clip(jax.random.normal(first, cube_shape, jnp.float32), -6.0, 6.0)
    trend = jnp.exp(math.log(3.0) * jnp.arange(NX).astype(jnp.float32) / NX)
    row_scale = jnp.exp(jax.random.uniform(second, (NX,), jnp.float32, 0.0, math.log(3.2)))
    column_scale = jnp.exp(jax.random.uniform(third, (NY,), jnp.float32, 0.0, math.log(3.2)))
    rough = jax.random.uniform(fourth, cube_shape, jnp.float32, 0.5, 1.5)
    return base * (trend * row_scale)[None, :, None] * column_scale[None, None, :] * rough


def draw_mask(key, part):
    key = jax.random.fold_in(key, 23)
    first, second = jax.random.split(key, 2)
    tiles_first = NX // CX
    tiles_second = NY // (CY // 2)
    tile_draw = jax.random.randint(first, (tiles_first, tiles_second), 0, 1000)
    threshold = 250 + 500 * jnp.arange(tiles_first) // tiles_first
    chosen = tile_draw < threshold[:, None]
    chosen = jnp.repeat(jnp.repeat(chosen, CX, axis=0), CY // 2, axis=1)
    voxel_draw = jax.random.randint(second, (PLANES, NX, NY), 0, 1000) < 800
    plane_ids = jnp.arange(PLANES)[:, None, None]
    first_ids = jnp.arange(NX)[None, :, None]
    second_ids = jnp.arange(NY)[None, None, :]
    forced = (plane_ids == 0) & (first_ids % 16 == 0) & (second_ids % 16 == 0)
    return (chosen[None, :, :] & voxel_draw | forced).astype(jnp.int32)


def setup_inputs(seed: int = 0, part: int = 0) -> dict:
    arg_keys = jax.random.split(jax.random.key(seed), 4)
    part_keys = jax.random.split(jax.random.fold_in(arg_keys[3], part), 4)
    volume = draw_volume(jax.random.fold_in(jax.random.fold_in(arg_keys[3], part), 71), part)
    mask = draw_mask(jax.random.fold_in(jax.random.fold_in(arg_keys[3], part), 71), part)
    res_index = jax.random.randint(part_keys[2], (2,), 0, 8).astype(jnp.int32)
    return {"volume": volume, "mask": mask, "res_index": res_index}


sigma_fine = 2.0
sigma_coarse = 3.5
sigma_depth = 1.5
wave_fine = 2.5
wave_coarse = 4.5
epsilon = 1e-06

def axis_kernels(window_sigma, frequency, reach):
    distance = jnp.arange(-reach, reach + 1).astype(jnp.float32)
    window = jnp.exp(-distance * distance / (2.0 * window_sigma * window_sigma))
    return (window, window * jnp.cos(frequency * distance), window * jnp.sin(frequency * distance))

def correlate(extended, kernels_side, kernels_depth, rows_here, columns_here):
    span = kernels_side[0].shape[0]
    depth_span = kernels_depth[0].shape[0]

    def along_y(kernel):
        summed = kernel[0] * extended[:, :, 0:columns_here]
        for offset in range(1, span):
            summed = summed + kernel[offset] * extended[:, :, offset:offset + columns_here]
        return summed

    def along_x(source, kernel):
        summed = kernel[0] * source[:, 0:rows_here, :]
        for offset in range(1, span):
            summed = summed + kernel[offset] * source[:, offset:offset + rows_here, :]
        return summed

    def along_z(source, kernel):
        planes_here = source.shape[0]
        padded = jnp.pad(source, ((ZREACH, ZREACH), (0, 0), (0, 0)))
        summed = kernel[0] * padded[0:planes_here]
        for offset in range(1, depth_span):
            summed = summed + kernel[offset] * padded[offset:offset + planes_here]
        return summed
    window_x, cosine_x, sine_x = kernels_side
    window_z, cosine_z, sine_z = kernels_depth
    window_y = along_y(window_x)
    cosine_y = along_y(cosine_x)
    sine_y = along_y(sine_x)
    flat = along_x(window_y, window_x)
    return [along_z(flat, window_z), along_z(along_x(window_y, cosine_x), window_z), along_z(along_x(window_y, sine_x), window_z), along_z(along_x(cosine_y, window_x), window_z), along_z(along_x(sine_y, window_x), window_z), along_z(flat, cosine_z), along_z(flat, sine_z)]

def whitening(window_sigma, frequency):
    side = jnp.arange(-HALO, HALO + 1).astype(jnp.float32)
    depth = jnp.arange(-ZREACH, ZREACH + 1).astype(jnp.float32)
    window_x = jnp.exp(-side * side / (2.0 * window_sigma * window_sigma))
    window_z = jnp.exp(-depth * depth / (2.0 * sigma_depth * sigma_depth))
    weight = window_z[:, None, None] * window_x[None, :, None] * window_x[None, None, :]
    cube_shape = weight.shape
    along_first = jnp.broadcast_to(side[None, :, None], cube_shape)
    along_second = jnp.broadcast_to(side[None, None, :], cube_shape)
    along_depth = jnp.broadcast_to(depth[:, None, None], cube_shape)
    basis_terms = jnp.stack([jnp.ones(cube_shape, jnp.float32), jnp.cos(frequency * along_first), jnp.sin(frequency * along_first), jnp.cos(frequency * along_second), jnp.sin(frequency * along_second), jnp.cos(frequency * along_depth), jnp.sin(frequency * along_depth)])
    gram_matrix = jnp.einsum('jzxy,kzxy->jk', basis_terms * weight, basis_terms, precision=lax.Precision.HIGHEST)
    factor_lower = jnp.linalg.cholesky(gram_matrix)
    identity = jnp.eye(7, dtype=jnp.float32)
    inverse_rows = []
    for position in range(7):
        row_value = identity[position]
        for earlier in range(position):
            row_value = row_value - factor_lower[position, earlier] * inverse_rows[earlier]
        inverse_rows.append(row_value / factor_lower[position, position])
    return inverse_rows

def statistic(extended, wave_index, window_sigma, wave_base, variance, rows_here, columns_here):
    frequency = 2.0 * math.pi / (wave_base + 0.25 * wave_index.astype(jnp.float32))
    kernels_side = axis_kernels(window_sigma, frequency, HALO)
    kernels_depth = axis_kernels(sigma_depth, frequency, ZREACH)
    responses = correlate(extended, kernels_side, kernels_depth, rows_here, columns_here)
    inverse_rows = whitening(window_sigma, frequency)
    summed = jnp.zeros(responses[0].shape, jnp.float32)
    for position in range(1, 7):
        projected = inverse_rows[position][0] * responses[0]
        for earlier in range(1, position + 1):
            projected = projected + inverse_rows[position][earlier] * responses[earlier]
        summed = summed + projected * projected
    return summed / (6.0 * variance)

def reference(volume, mask, res_index):
    weights = mask.astype(jnp.float32)
    counted = jnp.sum(weights)
    centre = jnp.sum(weights * volume) / counted
    deviation = volume - centre
    variance = jnp.sum(weights * deviation * deviation) / (counted - 1.0) + epsilon
    extended = jnp.pad(volume, ((0, 0), (HALO, HALO), (HALO, HALO)))
    rows_here = volume.shape[1]
    columns_here = volume.shape[2]
    fine_statistic = statistic(extended, res_index[0], sigma_fine, wave_fine, variance, rows_here, columns_here)
    coarse_statistic = statistic(extended, res_index[1], sigma_coarse, wave_coarse, variance, rows_here, columns_here)
    return (fine_statistic, coarse_statistic)
```

```python
import functools
import math

import jax
import jax.numpy as jnp
from jax import lax
from jax.experimental import pallas as pl
from jax.experimental.pallas import tpu as pltpu
from jax.sharding import PartitionSpec as P

HALO = 8
ZREACH = 2
LANES = 128
GROUP = 256
MESH = pl.DeviceIdType.MESH

sigma_fine = 2.0
sigma_coarse = 3.5
sigma_depth = 1.5
wave_fine = 2.5
wave_coarse = 4.5
epsilon = 1e-06
levels = ((sigma_fine, wave_fine), (sigma_coarse, wave_coarse))

RESPONSES = ((0, 0, 0), (0, 1, 0), (0, 2, 0), (0, 0, 1), (0, 0, 2), (1, 0, 0), (2, 0, 0))


def split(value):
    high = value.astype(jnp.bfloat16)
    low = (value - high.astype(jnp.float32)).astype(jnp.bfloat16)
    return high, low


def windows(distance, sigma, frequency, reach):
    inside = jnp.abs(distance) <= reach
    window = jnp.where(inside, jnp.exp(-distance * distance / (2.0 * sigma * sigma)), 0.0)
    angle = frequency * distance
    return window, window * jnp.cos(angle), window * jnp.sin(angle)


def whitening(side, depth):
    def total(value):
        return jnp.broadcast_to(jnp.sum(value, axis=1, keepdims=True), value.shape)

    def moments(weighted, plain):
        return {
            (j, k): total(weighted[j] * plain[k]) for j in range(3) for k in range(j, 3)
        }

    side_moment = moments(*side)
    depth_moment = moments(*depth)

    def gram(j, k):
        value = None
        for dim in range(3):
            pair = tuple(sorted((RESPONSES[j][dim], RESPONSES[k][dim])))
            factor = (depth_moment if dim == 0 else side_moment)[pair]
            value = factor if value is None else value * factor
        return value

    lower = [[None] * 7 for _ in range(7)]
    reciprocal = [None] * 7
    for k in range(7):
        pivot = gram(k, k)
        for m in range(k):
            pivot = pivot - lower[k][m] * lower[k][m]
        lower[k][k] = jnp.sqrt(pivot)
        reciprocal[k] = 1.0 / lower[k][k]
        for j in range(k + 1, 7):
            value = gram(j, k)
            for m in range(k):
                value = value - lower[j][m] * lower[k][m]
            lower[j][k] = value * reciprocal[k]
    inverse = [[None] * 7 for _ in range(7)]
    for j in range(7):
        for k in range(j + 1):
            if j == k:
                inverse[j][k] = reciprocal[j]
                continue
            value = None
            for m in range(k, j):
                term = lower[j][m] * inverse[m][k]
                value = term if value is None else value + term
            inverse[j][k] = -value * reciprocal[j]
    return inverse


def build_matrices(index_ref, planes, rows, tmat, bmat):
    out_rows = planes * rows
    sublane = lax.broadcasted_iota(jnp.int32, (8, LANES), 0)
    lane = lax.broadcasted_iota(jnp.int32, (8, LANES), 1)
    fine = sublane < 4
    index = jnp.where(fine, index_ref[0], index_ref[1]).astype(jnp.float32)
    frequency = 2.0 * math.pi / (jnp.where(fine, wave_fine, wave_coarse) + 0.25 * index)
    sigma = jnp.where(fine, sigma_fine, sigma_coarse)

    distance = (HALO - lane).astype(jnp.float32)
    side = windows(distance, sigma, frequency, HALO)
    ones = jnp.ones_like(distance)
    side_plain = (ones, jnp.cos(frequency * distance), jnp.sin(frequency * distance))
    depth_distance = (ZREACH - lane).astype(jnp.float32)
    depth = windows(depth_distance, sigma_depth, frequency, ZREACH)
    depth_plain = (
        ones,
        jnp.cos(frequency * depth_distance),
        jnp.sin(frequency * depth_distance),
    )
    inverse = whitening((side, side_plain), (depth, depth_plain))

    row = lax.broadcasted_iota(jnp.int32, (LANES, LANES), 0)
    column = lax.broadcasted_iota(jnp.int32, (LANES, LANES), 1)
    offset = row - HALO - column
    upper = jnp.abs(offset) <= HALO
    beneath = jnp.abs(offset + LANES) <= HALO
    for level in range(2):
        for kind in range(3):
            line = jnp.broadcast_to(side[kind][4 * level : 4 * level + 1], (LANES, LANES))
            rolled = pltpu.roll(line, LANES - 2 * HALO, 1, stride=1, stride_axis=0)
            lanes = pl.ds((level * 3 + kind) * LANES, LANES)
            for part, keep in enumerate((upper, beneath)):
                high, low = split(jnp.where(keep, rolled, 0.0))
                tmat[pl.ds(part * LANES, LANES), lanes] = high
                tmat[pl.ds((2 + part) * LANES, LANES), lanes] = low
                tmat[pl.ds((4 + part) * LANES, LANES), lanes] = high

    def place(shape, own_value, low_value, high_value):
        position = lax.broadcasted_iota(jnp.int32, shape, 1)
        halo_low = planes * rows
        halo_high = halo_low + planes * HALO
        return jnp.where(
            position < halo_low,
            own_value(position),
            jnp.where(
                position < halo_high,
                low_value(position - halo_low),
                high_value(position - halo_high),
            ),
        )

    width = planes * (rows + 2 * HALO)
    source_x = place(
        (rows, width),
        lambda p: lax.rem(p, rows),
        lambda p: lax.rem(p, HALO) - HALO,
        lambda p: lax.rem(p, HALO) + rows,
    )
    source_z = place(
        (8, width),
        lambda p: lax.div(p, rows),
        lambda p: lax.div(p, HALO),
        lambda p: lax.div(p, HALO),
    )
    step_x = (source_x - lax.broadcasted_iota(jnp.int32, (rows, width), 0)).astype(jnp.float32)
    step_z = (source_z - lax.broadcasted_iota(jnp.int32, (8, width), 0)).astype(jnp.float32)
    for level in range(2):
        line = slice(4 * level, 4 * level + 1)
        kernel_x = windows(step_x, levels[level][0], frequency[line], HALO)
        kernel_z = windows(step_z, sigma_depth, frequency[line], ZREACH)
        factors = {}
        for z_kind, x_kind, _ in RESPONSES:
            if (z_kind, x_kind) not in factors:
                factors[z_kind, x_kind] = jnp.concatenate(
                    [kernel_z[z_kind][z : z + 1] * kernel_x[x_kind] for z in range(planes)], axis=0
                )
        for j in range(1, 7):
            for kind in range(3):
                value = None
                for k in range(j + 1):
                    z_kind, x_kind, y_kind = RESPONSES[k]
                    if y_kind == kind:
                        term = inverse[j][k][line] * factors[z_kind, x_kind]
                        value = term if value is None else value + term
                if value is None:
                    value = jnp.zeros((out_rows, width), jnp.float32)
                high, low = split(value)
                lines = pl.ds((j - 1) * out_rows, out_rows)
                bmat[level, lines, pl.ds(kind * width, width)] = high
                bmat[level, lines, pl.ds((3 + kind) * width, width)] = low
                bmat[level, lines, pl.ds((6 + kind) * width, width)] = high


def kernel(
    ngx,
    ngy,
    index_ref,
    volume_ref,
    mask_ref,
    fine_ref,
    coarse_ref,
    own,
    halo,
    masked,
    tmat,
    bmat,
    result,
    scale,
    mine,
    others,
    local_sem,
    edge_sem,
    halo_send,
    halo_recv,
    stat_send,
    stat_recv,
    out_sem,
):
    planes, rows, columns = volume_ref.shape
    groups = columns // GROUP
    out_rows = planes * rows
    width = planes * (rows + 2 * HALO)
    devices = ngx * ngy
    gx = lax.axis_index("gx")
    gy = lax.axis_index("gy")
    me = gx * ngy + gy
    other = ngy - 1 - gy
    has_low = gx > 0
    has_high = gx < ngx - 1

    def peer(step):
        target = lax.rem(me + step, devices)
        return {"gx": lax.div(target, ngy), "gy": lax.rem(target, ngy)}

    barrier = pltpu.get_barrier_semaphore()

    def greet(step, carry):
        pl.semaphore_signal(barrier, inc=1, device_id=peer(step), device_id_type=MESH)
        return carry

    lax.fori_loop(1, devices, greet, 0)

    volume_copy = pltpu.make_async_copy(
        volume_ref, own.at[:, :, pl.ds(LANES, columns)], local_sem.at[0]
    )
    mask_copy = pltpu.make_async_copy(mask_ref, masked, local_sem.at[1])
    volume_copy.start()
    mask_copy.start()

    outside = pl.ds(pl.multiple_of(gy * (columns + LANES), LANES), LANES)
    own[:, :, outside] = jnp.zeros((planes, rows, LANES), jnp.float32)
    halo[:, :, :, outside] = jnp.zeros((2, planes, HALO, LANES), jnp.float32)

    @pl.when(jnp.logical_not(has_low))
    def _():
        halo[0] = jnp.zeros((planes, HALO, columns + 2 * LANES), jnp.float32)

    @pl.when(jnp.logical_not(has_high))
    def _():
        halo[1] = jnp.zeros((planes, HALO, columns + 2 * LANES), jnp.float32)

    def row_target(direction):
        return jnp.minimum(gx + 1, ngx - 1) if direction == 0 else jnp.maximum(gx - 1, 0)

    def rows_out(direction):
        return pl.ds(rows - HALO if direction == 0 else 0, HALO)

    edge_from = pl.ds(pl.multiple_of(other * (columns - LANES), LANES), LANES)
    edge_to = pl.ds(pl.multiple_of(gy * (columns + LANES), LANES), LANES)

    edge_copy = pltpu.make_async_remote_copy(
        src_ref=volume_ref.at[:, :, edge_from],
        dst_ref=own.at[:, :, edge_to],
        send_sem=edge_sem.at[0, 0],
        recv_sem=edge_sem.at[1, 0],
        device_id={"gy": other},
        device_id_type=MESH,
    )

    def corner_copy(direction):
        return pltpu.make_async_remote_copy(
            src_ref=volume_ref.at[:, rows_out(direction), edge_from],
            dst_ref=halo.at[direction, :, :, edge_to],
            send_sem=edge_sem.at[0, 1 + direction],
            recv_sem=edge_sem.at[1, 1 + direction],
            device_id={"gx": row_target(direction), "gy": other},
            device_id_type=MESH,
        )

    def halo_copy(direction, start, size, piece):
        return pltpu.make_async_remote_copy(
            src_ref=volume_ref.at[:, rows_out(direction), pl.ds(start, size)],
            dst_ref=halo.at[
                direction, :, :, pl.ds(pl.multiple_of(start + LANES, LANES), size)
            ],
            send_sem=halo_send.at[direction, piece],
            recv_sem=halo_recv.at[direction, piece],
            device_id={"gx": row_target(direction)},
            device_id_type=MESH,
        )

    def first_piece(direction):
        return halo_copy(direction, 0, LANES, 0)

    def middle_piece(direction, group):
        start = pl.multiple_of(group * GROUP + LANES, LANES)
        return halo_copy(direction, start, GROUP, group + 1)

    def last_piece(direction):
        return halo_copy(direction, columns - LANES, LANES, groups)

    sends_to = (has_high, has_low)
    gets_from = (has_low, has_high)

    pl.semaphore_wait(barrier, devices - 1)
    edge_copy.start()
    for direction in range(2):

        @pl.when(sends_to[direction])
        def _():
            corner_copy(direction).start()
            first_piece(direction).start()

    def send_middle(group, carry):
        for direction in range(2):

            @pl.when(sends_to[direction])
            def _():
                middle_piece(direction, group).start()

        return carry

    lax.fori_loop(0, groups - 1, send_middle, 0)
    for direction in range(2):

        @pl.when(sends_to[direction])
        def _():
            last_piece(direction).start()

    volume_copy.wait()
    mask_copy.wait()
    weights = masked[...].astype(jnp.float32)
    values = own[:, :, pl.ds(LANES, columns)]
    count = jnp.sum(weights)
    summed = jnp.sum(weights * values)
    deviation = values - summed / jnp.maximum(count, 1.0)
    squares = jnp.sum(weights * deviation * deviation)
    line = lax.broadcasted_iota(jnp.int32, (8, LANES), 0)
    mine[...] = jnp.where(line == 0, count, jnp.where(line == 1, summed, squares))

    def stat_copy(step):
        return pltpu.make_async_remote_copy(
            src_ref=mine,
            dst_ref=others.at[step - 1],
            send_sem=stat_send.at[step - 1],
            recv_sem=stat_recv.at[step - 1],
            device_id=peer(step),
            device_id_type=MESH,
        )

    def send_stat(step, carry):
        stat_copy(step).start()
        return carry

    lax.fori_loop(1, devices, send_stat, 0)

    build_matrices(index_ref, planes, rows, tmat, bmat)

    def wait_stat(step, carry):
        stat_copy(step).wait_recv()
        return carry

    lax.fori_loop(1, devices, wait_stat, 0)
    mine_now = mine[...]
    gathered = others[...]
    counts = gathered[:, 0, :]
    sums = gathered[:, 1, :]
    counted = mine_now[0:1] + jnp.sum(counts, axis=0, keepdims=True)
    centre = (mine_now[1:2] + jnp.sum(sums, axis=0, keepdims=True)) / counted
    apart = sums / jnp.maximum(counts, 1.0) - centre
    mine_apart = mine_now[1:2] / jnp.maximum(mine_now[0:1], 1.0) - centre
    spread = jnp.sum(gathered[:, 2, :] + counts * apart * apart, axis=0, keepdims=True) + (
        mine_now[2:3] + mine_now[0:1] * mine_apart * mine_apart
    )
    variance = spread / (counted - 1.0) + epsilon
    scale[...] = jnp.broadcast_to(1.0 / (6.0 * variance), (8, LANES))

    edge_copy.wait_recv()
    for direction in range(2):

        @pl.when(gets_from[direction])
        def _():
            corner_copy(direction).wait_recv()
            first_piece(direction).wait_recv()

    outputs = (fine_ref, coarse_ref)

    def out_copy(level, group):
        lanes = pl.ds(pl.multiple_of(group * GROUP, GROUP), GROUP)
        return pltpu.make_async_copy(
            result.at[level, :, :, lanes],
            outputs[level].at[:, :, lanes],
            out_sem.at[level, group],
        )

    def body(group, carry):
        for direction in range(2):

            @pl.when(jnp.logical_and(gets_from[direction], group < groups - 1))
            def _():
                middle_piece(direction, jnp.minimum(group, groups - 2)).wait_recv()

            @pl.when(jnp.logical_and(gets_from[direction], group == groups - 1))
            def _():
                last_piece(direction).wait_recv()

        start = pl.multiple_of(group * GROUP, GROUP)
        load = pl.ds(start, GROUP + 2 * LANES)
        block = jnp.concatenate(
            [
                own[:, :, load].reshape(out_rows, GROUP + 2 * LANES),
                halo[:, :, :, load].reshape(2 * planes * HALO, GROUP + 2 * LANES),
            ],
            axis=0,
        )[:, LANES - HALO : GROUP + 2 * LANES - HALO]
        high, low = split(block)
        left = jnp.concatenate(
            [
                jnp.concatenate([part[:, s : s + GROUP] for part in (high, high, low)], axis=1)
                for s in (0, LANES)
            ],
            axis=0,
        )
        along_y = jnp.dot(left, tmat[...], preferred_element_type=jnp.float32)
        for level in range(2):
            kinds = [
                jnp.concatenate(
                    [
                        along_y[
                            s * width : (s + 1) * width,
                            (level * 3 + kind) * LANES : (level * 3 + kind + 1) * LANES,
                        ]
                        for s in range(2)
                    ],
                    axis=1,
                )
                for kind in range(3)
            ]
            high, low = split(jnp.concatenate(kinds, axis=0))
            projected = jnp.dot(
                bmat[level],
                jnp.concatenate([high, high, low], axis=0),
                preferred_element_type=jnp.float32,
            )
            total = None
            for j in range(6):
                part = projected[j * out_rows : (j + 1) * out_rows]
                total = part * part if total is None else total + part * part
            total = total * jnp.concatenate([scale[0:1], scale[0:1]], axis=1)
            result[level, :, :, pl.ds(start, GROUP)] = total.reshape(planes, rows, GROUP)
            out_copy(level, group).start()
        return carry

    lax.fori_loop(0, groups, body, 0)

    edge_copy.wait_send()
    for direction in range(2):

        @pl.when(sends_to[direction])
        def _():
            corner_copy(direction).wait_send()
            first_piece(direction).wait_send()
            last_piece(direction).wait_send()

    def end_middle(group, carry):
        for direction in range(2):

            @pl.when(sends_to[direction])
            def _():
                middle_piece(direction, group).wait_send()

        return carry

    lax.fori_loop(0, groups - 1, end_middle, 0)

    def end_stat(step, carry):
        stat_copy(step).wait_send()
        return carry

    lax.fori_loop(1, devices, end_stat, 0)

    def end_out(group, carry):
        for level in range(2):
            out_copy(level, group).wait()
        return carry

    lax.fori_loop(0, groups, end_out, 0)


def per_device(volume, mask, res_index):
    planes, rows, columns = volume.shape
    ngx = lax.axis_size("gx")
    ngy = lax.axis_size("gy")
    devices = ngx * ngy
    groups = columns // GROUP
    width = planes * (rows + 2 * HALO)
    extended = columns + 2 * LANES
    out = jax.ShapeDtypeStruct(volume.shape, jnp.float32)
    return pl.pallas_call(
        functools.partial(kernel, ngx, ngy),
        out_shape=(out, out),
        in_specs=[
            pl.BlockSpec(memory_space=pltpu.SMEM),
            pl.BlockSpec(memory_space=pl.ANY),
            pl.BlockSpec(memory_space=pl.ANY),
        ],
        out_specs=(pl.BlockSpec(memory_space=pl.ANY), pl.BlockSpec(memory_space=pl.ANY)),
        scratch_shapes=[
            pltpu.VMEM((planes, rows, extended), jnp.float32),
            pltpu.VMEM((2, planes, HALO, extended), jnp.float32),
            pltpu.VMEM((planes, rows, columns), jnp.int32),
            pltpu.VMEM((6 * LANES, 6 * LANES), jnp.bfloat16),
            pltpu.VMEM((2, 6 * planes * rows, 9 * width), jnp.bfloat16),
            pltpu.VMEM((2, planes, rows, columns), jnp.float32),
            pltpu.VMEM((8, LANES), jnp.float32),
            pltpu.VMEM((8, LANES), jnp.float32),
            pltpu.VMEM((devices - 1, 8, LANES), jnp.float32),
            pltpu.SemaphoreType.DMA((2,)),
            pltpu.SemaphoreType.DMA((2, 3)),
            pltpu.SemaphoreType.DMA((2, groups + 1)),
            pltpu.SemaphoreType.DMA((2, groups + 1)),
            pltpu.SemaphoreType.DMA((devices - 1,)),
            pltpu.SemaphoreType.DMA((devices - 1,)),
            pltpu.SemaphoreType.DMA((2, groups)),
        ],
        compiler_params=pltpu.CompilerParams(
            collective_id=0, has_side_effects=True, vmem_limit_bytes=40 * 1024 * 1024
        ),
        cost_estimate=pl.CostEstimate(
            flops=6_000_000_000, bytes_accessed=2_500_000, transcendentals=100_000
        ),
        name="resolution_statistic",
    )(res_index, volume, mask)


def solution(mesh):
    placed = (P(None, ("parts", "gx"), "gy"), P(None, ("parts", "gx"), "gy"), P("parts"))
    return jax.shard_map(
        per_device,
        mesh=mesh,
        in_specs=placed,
        out_specs=(P(None, ("parts", "gx"), "gy"), P(None, ("parts", "gx"), "gy")),
        check_vma=False,
    )
```

```python
import functools
import math

import jax
import jax.numpy as jnp
from jax import lax
from jax.experimental import pallas as pl
from jax.experimental.pallas import tpu as pltpu
from jax.sharding import PartitionSpec as P

HALO = 8
ZREACH = 2
LANES = 128
GROUP = 512
MESH = pl.DeviceIdType.MESH

sigma_fine = 2.0
sigma_coarse = 3.5
sigma_depth = 1.5
wave_fine = 2.5
wave_coarse = 4.5
epsilon = 1e-06
levels = ((sigma_fine, wave_fine), (sigma_coarse, wave_coarse))

RESPONSES = ((0, 0, 0), (0, 1, 0), (0, 2, 0), (0, 0, 1), (0, 0, 2), (1, 0, 0), (2, 0, 0))


def split(value):
    high = value.astype(jnp.bfloat16)
    low = (value - high.astype(jnp.float32)).astype(jnp.bfloat16)
    return high, low


def windows(distance, sigma, frequency, reach):
    inside = jnp.abs(distance) <= reach
    window = jnp.where(inside, jnp.exp(-distance * distance / (2.0 * sigma * sigma)), 0.0)
    angle = frequency * distance
    return window, window * jnp.cos(angle), window * jnp.sin(angle)


def whitening(side, depth):
    def total(value):
        return jnp.broadcast_to(jnp.sum(value, axis=1, keepdims=True), value.shape)

    def moments(weighted, plain):
        return {
            (j, k): total(weighted[j] * plain[k]) for j in range(3) for k in range(j, 3)
        }

    side_moment = moments(*side)
    depth_moment = moments(*depth)

    def gram(j, k):
        value = None
        for dim in range(3):
            pair = tuple(sorted((RESPONSES[j][dim], RESPONSES[k][dim])))
            factor = (depth_moment if dim == 0 else side_moment)[pair]
            value = factor if value is None else value * factor
        return value

    lower = [[None] * 7 for _ in range(7)]
    reciprocal = [None] * 7
    for k in range(7):
        pivot = gram(k, k)
        for m in range(k):
            pivot = pivot - lower[k][m] * lower[k][m]
        lower[k][k] = jnp.sqrt(pivot)
        reciprocal[k] = 1.0 / lower[k][k]
        for j in range(k + 1, 7):
            value = gram(j, k)
            for m in range(k):
                value = value - lower[j][m] * lower[k][m]
            lower[j][k] = value * reciprocal[k]
    inverse = [[None] * 7 for _ in range(7)]
    for j in range(7):
        for k in range(j + 1):
            if j == k:
                inverse[j][k] = reciprocal[j]
                continue
            value = None
            for m in range(k, j):
                term = lower[j][m] * inverse[m][k]
                value = term if value is None else value + term
            inverse[j][k] = -value * reciprocal[j]
    return inverse


def build_matrices(index_ref, planes, rows, tmat, bmat):
    out_rows = planes * rows
    sublane = lax.broadcasted_iota(jnp.int32, (8, LANES), 0)
    lane = lax.broadcasted_iota(jnp.int32, (8, LANES), 1)
    fine = sublane < 4
    index = jnp.where(fine, index_ref[0], index_ref[1]).astype(jnp.float32)
    frequency = 2.0 * math.pi / (jnp.where(fine, wave_fine, wave_coarse) + 0.25 * index)
    sigma = jnp.where(fine, sigma_fine, sigma_coarse)

    distance = (HALO - lane).astype(jnp.float32)
    side = windows(distance, sigma, frequency, HALO)
    ones = jnp.ones_like(distance)
    side_plain = (ones, jnp.cos(frequency * distance), jnp.sin(frequency * distance))
    depth_distance = (ZREACH - lane).astype(jnp.float32)
    depth = windows(depth_distance, sigma_depth, frequency, ZREACH)
    depth_plain = (
        ones,
        jnp.cos(frequency * depth_distance),
        jnp.sin(frequency * depth_distance),
    )
    inverse = whitening((side, side_plain), (depth, depth_plain))

    row = lax.broadcasted_iota(jnp.int32, (LANES, LANES), 0)
    column = lax.broadcasted_iota(jnp.int32, (LANES, LANES), 1)
    offset = row - HALO - column
    upper = jnp.abs(offset) <= HALO
    beneath = jnp.abs(offset + LANES) <= HALO
    for level in range(2):
        for kind in range(3):
            line = jnp.broadcast_to(side[kind][4 * level : 4 * level + 1], (LANES, LANES))
            rolled = pltpu.roll(line, LANES - 2 * HALO, 1, stride=1, stride_axis=0)
            lanes = pl.ds((level * 3 + kind) * LANES, LANES)
            for part, keep in enumerate((upper, beneath)):
                high, low = split(jnp.where(keep, rolled, 0.0))
                tmat[pl.ds(part * LANES, LANES), lanes] = high
                tmat[pl.ds((2 + part) * LANES, LANES), lanes] = low
                tmat[pl.ds((4 + part) * LANES, LANES), lanes] = high

    def place(shape, own_value, low_value, high_value):
        position = lax.broadcasted_iota(jnp.int32, shape, 1)
        halo_low = planes * rows
        halo_high = halo_low + planes * HALO
        return jnp.where(
            position < halo_low,
            own_value(position),
            jnp.where(
                position < halo_high,
                low_value(position - halo_low),
                high_value(position - halo_high),
            ),
        )

    width = planes * (rows + 2 * HALO)
    source_x = place(
        (rows, width),
        lambda p: lax.rem(p, rows),
        lambda p: lax.rem(p, HALO) - HALO,
        lambda p: lax.rem(p, HALO) + rows,
    )
    source_z = place(
        (8, width),
        lambda p: lax.div(p, rows),
        lambda p: lax.div(p, HALO),
        lambda p: lax.div(p, HALO),
    )
    step_x = (source_x - lax.broadcasted_iota(jnp.int32, (rows, width), 0)).astype(jnp.float32)
    step_z = (source_z - lax.broadcasted_iota(jnp.int32, (8, width), 0)).astype(jnp.float32)
    for level in range(2):
        line = slice(4 * level, 4 * level + 1)
        kernel_x = windows(step_x, levels[level][0], frequency[line], HALO)
        kernel_z = windows(step_z, sigma_depth, frequency[line], ZREACH)
        factors = {}
        for z_kind, x_kind, _ in RESPONSES:
            if (z_kind, x_kind) not in factors:
                factors[z_kind, x_kind] = jnp.concatenate(
                    [kernel_z[z_kind][z : z + 1] * kernel_x[x_kind] for z in range(planes)], axis=0
                )
        for j in range(1, 7):
            for kind in range(3):
                value = None
                for k in range(j + 1):
                    z_kind, x_kind, y_kind = RESPONSES[k]
                    if y_kind == kind:
                        term = inverse[j][k][line] * factors[z_kind, x_kind]
                        value = term if value is None else value + term
                if value is None:
                    value = jnp.zeros((out_rows, width), jnp.float32)
                high, low = split(value)
                lines = pl.ds((j - 1) * out_rows, out_rows)
                bmat[level, lines, pl.ds(kind * width, width)] = high
                bmat[level, lines, pl.ds((3 + kind) * width, width)] = low
                bmat[level, lines, pl.ds((6 + kind) * width, width)] = high


def kernel(
    ngx,
    ngy,
    index_ref,
    volume_ref,
    mask_ref,
    raw_ref,
    scale_ref,
    own,
    halo,
    masked,
    tmat,
    bmat,
    result,
    mine,
    others,
    local_sem,
    edge_sem,
    halo_send,
    halo_recv,
    stat_send,
    stat_recv,
    out_sem,
):
    planes, rows, columns = volume_ref.shape
    groups = columns // GROUP
    out_rows = planes * rows
    width = planes * (rows + 2 * HALO)
    devices = ngx * ngy
    gx = lax.axis_index("gx")
    gy = lax.axis_index("gy")
    me = gx * ngy + gy
    other = ngy - 1 - gy
    has_low = gx > 0
    has_high = gx < ngx - 1

    def peer(step):
        target = lax.rem(me + step, devices)
        return {"gx": lax.div(target, ngy), "gy": lax.rem(target, ngy)}

    barrier = pltpu.get_barrier_semaphore()

    def greet(step, carry):
        pl.semaphore_signal(barrier, inc=1, device_id=peer(step), device_id_type=MESH)
        return carry

    lax.fori_loop(1, devices, greet, 0)

    volume_copy = pltpu.make_async_copy(
        volume_ref, own.at[:, :, pl.ds(LANES, columns)], local_sem.at[0]
    )
    mask_copy = pltpu.make_async_copy(mask_ref, masked, local_sem.at[1])
    volume_copy.start()
    mask_copy.start()

    outside = pl.ds(pl.multiple_of(gy * (columns + LANES), LANES), LANES)
    own[:, :, outside] = jnp.zeros((planes, rows, LANES), jnp.float32)
    halo[:, :, :, outside] = jnp.zeros((2, planes, HALO, LANES), jnp.float32)

    @pl.when(jnp.logical_not(has_low))
    def _():
        halo[0] = jnp.zeros((planes, HALO, columns + 2 * LANES), jnp.float32)

    @pl.when(jnp.logical_not(has_high))
    def _():
        halo[1] = jnp.zeros((planes, HALO, columns + 2 * LANES), jnp.float32)

    def row_target(direction):
        return jnp.minimum(gx + 1, ngx - 1) if direction == 0 else jnp.maximum(gx - 1, 0)

    def rows_out(direction):
        return pl.ds(rows - HALO if direction == 0 else 0, HALO)

    edge_from = pl.ds(pl.multiple_of(other * (columns - LANES), LANES), LANES)
    edge_to = pl.ds(pl.multiple_of(gy * (columns + LANES), LANES), LANES)

    edge_copy = pltpu.make_async_remote_copy(
        src_ref=volume_ref.at[:, :, edge_from],
        dst_ref=own.at[:, :, edge_to],
        send_sem=edge_sem.at[0, 0],
        recv_sem=edge_sem.at[1, 0],
        device_id={"gy": other},
        device_id_type=MESH,
    )

    def corner_copy(direction):
        return pltpu.make_async_remote_copy(
            src_ref=volume_ref.at[:, rows_out(direction), edge_from],
            dst_ref=halo.at[direction, :, :, edge_to],
            send_sem=edge_sem.at[0, 1 + direction],
            recv_sem=edge_sem.at[1, 1 + direction],
            device_id={"gx": row_target(direction), "gy": other},
            device_id_type=MESH,
        )

    def halo_copy(direction, start, size, piece):
        return pltpu.make_async_remote_copy(
            src_ref=volume_ref.at[:, rows_out(direction), pl.ds(start, size)],
            dst_ref=halo.at[
                direction, :, :, pl.ds(pl.multiple_of(start + LANES, LANES), size)
            ],
            send_sem=halo_send.at[direction, piece],
            recv_sem=halo_recv.at[direction, piece],
            device_id={"gx": row_target(direction)},
            device_id_type=MESH,
        )

    def first_piece(direction):
        return halo_copy(direction, 0, LANES, 0)

    def middle_piece(direction, group):
        start = pl.multiple_of(group * GROUP + LANES, LANES)
        return halo_copy(direction, start, GROUP, group + 1)

    def last_piece(direction):
        return halo_copy(direction, columns - GROUP + LANES, GROUP - LANES, groups)

    sends_to = (has_high, has_low)
    gets_from = (has_low, has_high)

    build_matrices(index_ref, planes, rows, tmat, bmat)
    pl.semaphore_wait(barrier, devices - 1)
    edge_copy.start()
    for direction in range(2):

        @pl.when(sends_to[direction])
        def _():
            corner_copy(direction).start()
            first_piece(direction).start()

    def send_middle(group, carry):
        for direction in range(2):

            @pl.when(sends_to[direction])
            def _():
                middle_piece(direction, group).start()

        return carry

    lax.fori_loop(0, groups - 1, send_middle, 0)
    for direction in range(2):

        @pl.when(sends_to[direction])
        def _():
            last_piece(direction).start()

    volume_copy.wait()
    mask_copy.wait()
    weights = masked[...].astype(jnp.float32)
    values = own[:, :, pl.ds(LANES, columns)]
    count = jnp.sum(weights)
    summed = jnp.sum(weights * values)
    deviation = values - summed / jnp.maximum(count, 1.0)
    squares = jnp.sum(weights * deviation * deviation)
    line = lax.broadcasted_iota(jnp.int32, (8, LANES), 0)
    mine[...] = jnp.where(line == 0, count, jnp.where(line == 1, summed, squares))

    def stat_copy(step):
        return pltpu.make_async_remote_copy(
            src_ref=mine,
            dst_ref=others.at[step - 1],
            send_sem=stat_send.at[step - 1],
            recv_sem=stat_recv.at[step - 1],
            device_id=peer(step),
            device_id_type=MESH,
        )

    def send_stat(step, carry):
        stat_copy(step).start()
        return carry

    lax.fori_loop(1, devices, send_stat, 0)


    edge_copy.wait_recv()
    for direction in range(2):

        @pl.when(gets_from[direction])
        def _():
            corner_copy(direction).wait_recv()
            first_piece(direction).wait_recv()

    def out_copy(level, group):
        lanes = pl.ds(pl.multiple_of(group * GROUP, GROUP), GROUP)
        return pltpu.make_async_copy(
            result.at[level, :, :, lanes],
            raw_ref.at[level, :, :, lanes],
            out_sem.at[level, group],
        )

    def body(group, carry):
        for direction in range(2):

            @pl.when(jnp.logical_and(gets_from[direction], group < groups - 1))
            def _():
                middle_piece(direction, jnp.minimum(group, groups - 2)).wait_recv()

            @pl.when(jnp.logical_and(gets_from[direction], group == groups - 1))
            def _():
                last_piece(direction).wait_recv()

        start = pl.multiple_of(group * GROUP, GROUP)
        load = pl.ds(start, GROUP + 2 * LANES)
        block = jnp.concatenate(
            [
                own[:, :, load].reshape(out_rows, GROUP + 2 * LANES),
                halo[:, :, :, load].reshape(2 * planes * HALO, GROUP + 2 * LANES),
            ],
            axis=0,
        )[:, LANES - HALO : GROUP + 2 * LANES - HALO]
        high, low = split(block)
        left = jnp.concatenate(
            [
                jnp.concatenate([part[:, s : s + 2 * LANES] for part in (high, high, low)], axis=1)
                for s in range(0, GROUP, LANES)
            ],
            axis=0,
        )
        along_y = jnp.dot(left, tmat[...], preferred_element_type=jnp.float32)
        for level in range(2):
            kinds = [
                jnp.concatenate(
                    [
                        along_y[
                            s * width : (s + 1) * width,
                            (level * 3 + kind) * LANES : (level * 3 + kind + 1) * LANES,
                        ]
                        for s in range(GROUP // LANES)
                    ],
                    axis=1,
                )
                for kind in range(3)
            ]
            high, low = split(jnp.concatenate(kinds, axis=0))
            projected = jnp.dot(
                bmat[level],
                jnp.concatenate([high, high, low], axis=0),
                preferred_element_type=jnp.float32,
            )
            total = None
            for j in range(6):
                part = projected[j * out_rows : (j + 1) * out_rows]
                total = part * part if total is None else total + part * part
            result[level, :, :, pl.ds(start, GROUP)] = total.reshape(planes, rows, GROUP)
            out_copy(level, group).start()
        return carry

    lax.fori_loop(0, groups, body, 0)

    def wait_stat(step, carry):
        stat_copy(step).wait_recv()
        return carry

    lax.fori_loop(1, devices, wait_stat, 0)
    mine_now = mine[...]
    gathered = others[...]
    counts = gathered[:, 0, :]
    sums = gathered[:, 1, :]
    counted = mine_now[0:1] + jnp.sum(counts, axis=0, keepdims=True)
    centre = (mine_now[1:2] + jnp.sum(sums, axis=0, keepdims=True)) / counted
    apart = sums / jnp.maximum(counts, 1.0) - centre
    mine_apart = mine_now[1:2] / jnp.maximum(mine_now[0:1], 1.0) - centre
    spread = jnp.sum(gathered[:, 2, :] + counts * apart * apart, axis=0, keepdims=True) + (
        mine_now[2:3] + mine_now[0:1] * mine_apart * mine_apart
    )
    variance = spread / (counted - 1.0) + epsilon
    scale_ref[...] = jnp.broadcast_to(1.0 / (6.0 * variance), (8, LANES))

    edge_copy.wait_send()
    for direction in range(2):

        @pl.when(sends_to[direction])
        def _():
            corner_copy(direction).wait_send()
            first_piece(direction).wait_send()
            last_piece(direction).wait_send()

    def end_middle(group, carry):
        for direction in range(2):

            @pl.when(sends_to[direction])
            def _():
                middle_piece(direction, group).wait_send()

        return carry

    lax.fori_loop(0, groups - 1, end_middle, 0)

    def end_stat(step, carry):
        stat_copy(step).wait_send()
        return carry

    lax.fori_loop(1, devices, end_stat, 0)

    def end_out(group, carry):
        for level in range(2):
            out_copy(level, group).wait()
        return carry

    lax.fori_loop(0, groups, end_out, 0)


def scale_kernel(factor_ref, raw_ref, fine_ref, coarse_ref):
    factor = factor_ref[0:1, 0:1].reshape(1, 1, 1)
    fine_ref[...] = raw_ref[0] * factor
    coarse_ref[...] = raw_ref[1] * factor


def per_device(volume, mask, res_index):
    planes, rows, columns = volume.shape
    ngx = lax.axis_size("gx")
    ngy = lax.axis_size("gy")
    devices = ngx * ngy
    groups = columns // GROUP
    width = planes * (rows + 2 * HALO)
    extended = columns + 2 * LANES
    out = jax.ShapeDtypeStruct(volume.shape, jnp.float32)
    raw, factor = pl.pallas_call(
        functools.partial(kernel, ngx, ngy),
        out_shape=(
            jax.ShapeDtypeStruct((2,) + volume.shape, jnp.float32),
            jax.ShapeDtypeStruct((8, LANES), jnp.float32),
        ),
        in_specs=[
            pl.BlockSpec(memory_space=pltpu.SMEM),
            pl.BlockSpec(memory_space=pl.ANY),
            pl.BlockSpec(memory_space=pl.ANY),
        ],
        out_specs=(
            pl.BlockSpec(memory_space=pl.ANY),
            pl.BlockSpec(memory_space=pltpu.VMEM),
        ),
        scratch_shapes=[
            pltpu.VMEM((planes, rows, extended), jnp.float32),
            pltpu.VMEM((2, planes, HALO, extended), jnp.float32),
            pltpu.VMEM((planes, rows, columns), jnp.int32),
            pltpu.VMEM((6 * LANES, 6 * LANES), jnp.bfloat16),
            pltpu.VMEM((2, 6 * planes * rows, 9 * width), jnp.bfloat16),
            pltpu.VMEM((2, planes, rows, columns), jnp.float32),
            pltpu.VMEM((8, LANES), jnp.float32),
            pltpu.VMEM((devices - 1, 8, LANES), jnp.float32),
            pltpu.SemaphoreType.DMA((2,)),
            pltpu.SemaphoreType.DMA((2, 3)),
            pltpu.SemaphoreType.DMA((2, groups + 1)),
            pltpu.SemaphoreType.DMA((2, groups + 1)),
            pltpu.SemaphoreType.DMA((devices - 1,)),
            pltpu.SemaphoreType.DMA((devices - 1,)),
            pltpu.SemaphoreType.DMA((2, groups)),
        ],
        compiler_params=pltpu.CompilerParams(
            collective_id=0, has_side_effects=True, vmem_limit_bytes=60 * 1024 * 1024
        ),
        cost_estimate=pl.CostEstimate(
            flops=6_000_000_000, bytes_accessed=2_500_000, transcendentals=100_000
        ),
        name="resolution_statistic",
    )(res_index, volume, mask)

    block = pl.BlockSpec((planes, rows, columns // 2), lambda i: (0, 0, i))
    return pl.pallas_call(
        scale_kernel,
        grid=(2,),
        out_shape=(out, out),
        in_specs=[
            pl.BlockSpec((8, LANES), lambda i: (0, 0)),
            pl.BlockSpec((2, planes, rows, columns // 2), lambda i: (0, 0, 0, i)),
        ],
        out_specs=(block, block),
        name="scale_statistic",
    )(factor, raw)


def solution(mesh):
    placed = (P(None, ("parts", "gx"), "gy"), P(None, ("parts", "gx"), "gy"), P("parts"))
    return jax.shard_map(
        per_device,
        mesh=mesh,
        in_specs=placed,
        out_specs=(P(None, ("parts", "gx"), "gy"), P(None, ("parts", "gx"), "gy")),
        check_vma=False,
    )
```

```python
import functools
import math

import jax
import jax.numpy as jnp
from jax import lax
from jax.experimental import pallas as pl
from jax.experimental.pallas import tpu as pltpu
from jax.sharding import PartitionSpec as P

HALO = 8
ZREACH = 2
LANES = 128
GROUP = 512
MESH = pl.DeviceIdType.MESH

sigma_fine = 2.0
sigma_coarse = 3.5
sigma_depth = 1.5
wave_fine = 2.5
wave_coarse = 4.5
epsilon = 1e-06
levels = ((sigma_fine, wave_fine), (sigma_coarse, wave_coarse))

RESPONSES = ((0, 0, 0), (0, 1, 0), (0, 2, 0), (0, 0, 1), (0, 0, 2), (1, 0, 0), (2, 0, 0))


def split(value):
    high = value.astype(jnp.bfloat16)
    low = (value - high.astype(jnp.float32)).astype(jnp.bfloat16)
    return high, low


def windows(distance, sigma, frequency, reach):
    inside = jnp.abs(distance) <= reach
    window = jnp.where(inside, jnp.exp(-distance * distance / (2.0 * sigma * sigma)), 0.0)
    angle = frequency * distance
    return window, window * jnp.cos(angle), window * jnp.sin(angle)


def whitening(side, depth):
    def total(value):
        return jnp.broadcast_to(jnp.sum(value, axis=1, keepdims=True), value.shape)

    def moments(weighted, plain):
        return {
            (j, k): total(weighted[j] * plain[k]) for j in range(3) for k in range(j, 3)
        }

    side_moment = moments(*side)
    depth_moment = moments(*depth)

    def gram(j, k):
        value = None
        for dim in range(3):
            pair = tuple(sorted((RESPONSES[j][dim], RESPONSES[k][dim])))
            factor = (depth_moment if dim == 0 else side_moment)[pair]
            value = factor if value is None else value * factor
        return value

    lower = [[None] * 7 for _ in range(7)]
    reciprocal = [None] * 7
    for k in range(7):
        pivot = gram(k, k)
        for m in range(k):
            pivot = pivot - lower[k][m] * lower[k][m]
        lower[k][k] = jnp.sqrt(pivot)
        reciprocal[k] = 1.0 / lower[k][k]
        for j in range(k + 1, 7):
            value = gram(j, k)
            for m in range(k):
                value = value - lower[j][m] * lower[k][m]
            lower[j][k] = value * reciprocal[k]
    inverse = [[None] * 7 for _ in range(7)]
    for j in range(7):
        for k in range(j + 1):
            if j == k:
                inverse[j][k] = reciprocal[j]
                continue
            value = None
            for m in range(k, j):
                term = lower[j][m] * inverse[m][k]
                value = term if value is None else value + term
            inverse[j][k] = -value * reciprocal[j]
    return inverse


def build_matrices(index_ref, planes, rows, tmat, bmat):
    out_rows = planes * rows
    sublane = lax.broadcasted_iota(jnp.int32, (8, LANES), 0)
    lane = lax.broadcasted_iota(jnp.int32, (8, LANES), 1)
    fine = sublane < 4
    index = jnp.where(fine, index_ref[0], index_ref[1]).astype(jnp.float32)
    frequency = 2.0 * math.pi / (jnp.where(fine, wave_fine, wave_coarse) + 0.25 * index)
    sigma = jnp.where(fine, sigma_fine, sigma_coarse)

    distance = (HALO - lane).astype(jnp.float32)
    side = windows(distance, sigma, frequency, HALO)
    ones = jnp.ones_like(distance)
    side_plain = (ones, jnp.cos(frequency * distance), jnp.sin(frequency * distance))
    depth_distance = (ZREACH - lane).astype(jnp.float32)
    depth = windows(depth_distance, sigma_depth, frequency, ZREACH)
    depth_plain = (
        ones,
        jnp.cos(frequency * depth_distance),
        jnp.sin(frequency * depth_distance),
    )
    inverse = whitening((side, side_plain), (depth, depth_plain))

    row = lax.broadcasted_iota(jnp.int32, (LANES, LANES), 0)
    column = lax.broadcasted_iota(jnp.int32, (LANES, LANES), 1)
    offset = row - HALO - column
    upper = jnp.abs(offset) <= HALO
    beneath = jnp.abs(offset + LANES) <= HALO
    for level in range(2):
        for kind in range(3):
            line = jnp.broadcast_to(side[kind][4 * level : 4 * level + 1], (LANES, LANES))
            rolled = pltpu.roll(line, LANES - 2 * HALO, 1, stride=1, stride_axis=0)
            lanes = pl.ds((level * 3 + kind) * LANES, LANES)
            for part, keep in enumerate((upper, beneath)):
                high, low = split(jnp.where(keep, rolled, 0.0))
                tmat[pl.ds(part * LANES, LANES), lanes] = high
                tmat[pl.ds((2 + part) * LANES, LANES), lanes] = low
                tmat[pl.ds((4 + part) * LANES, LANES), lanes] = high

    def place(shape, own_value, low_value, high_value):
        position = lax.broadcasted_iota(jnp.int32, shape, 1)
        halo_low = planes * rows
        halo_high = halo_low + planes * HALO
        return jnp.where(
            position < halo_low,
            own_value(position),
            jnp.where(
                position < halo_high,
                low_value(position - halo_low),
                high_value(position - halo_high),
            ),
        )

    width = planes * (rows + 2 * HALO)
    source_x = place(
        (rows, width),
        lambda p: lax.rem(p, rows),
        lambda p: lax.rem(p, HALO) - HALO,
        lambda p: lax.rem(p, HALO) + rows,
    )
    source_z = place(
        (8, width),
        lambda p: lax.div(p, rows),
        lambda p: lax.div(p, HALO),
        lambda p: lax.div(p, HALO),
    )
    step_x = (source_x - lax.broadcasted_iota(jnp.int32, (rows, width), 0)).astype(jnp.float32)
    step_z = (source_z - lax.broadcasted_iota(jnp.int32, (8, width), 0)).astype(jnp.float32)
    for level in range(2):
        line = slice(4 * level, 4 * level + 1)
        kernel_x = windows(step_x, levels[level][0], frequency[line], HALO)
        kernel_z = windows(step_z, sigma_depth, frequency[line], ZREACH)
        factors = {}
        for z_kind, x_kind, _ in RESPONSES:
            if (z_kind, x_kind) not in factors:
                factors[z_kind, x_kind] = jnp.concatenate(
                    [kernel_z[z_kind][z : z + 1] * kernel_x[x_kind] for z in range(planes)], axis=0
                )
        for j in range(1, 7):
            for kind in range(3):
                value = None
                for k in range(j + 1):
                    z_kind, x_kind, y_kind = RESPONSES[k]
                    if y_kind == kind:
                        term = inverse[j][k][line] * factors[z_kind, x_kind]
                        value = term if value is None else value + term
                if value is None:
                    value = jnp.zeros((out_rows, width), jnp.float32)
                high, low = split(value)
                lines = pl.ds((j - 1) * out_rows, out_rows)
                bmat[level, lines, pl.ds(kind * width, width)] = high
                bmat[level, lines, pl.ds((3 + kind) * width, width)] = low
                bmat[level, lines, pl.ds((6 + kind) * width, width)] = high


def kernel(
    ngx,
    ngy,
    index_ref,
    volume_ref,
    mask_ref,
    raw_ref,
    scale_ref,
    own,
    halo,
    masked,
    tmat,
    bmat,
    result,
    mine,
    others,
    local_sem,
    edge_sem,
    halo_send,
    halo_recv,
    stat_send,
    stat_recv,
    out_sem,
):
    planes, rows, columns = volume_ref.shape
    groups = columns // GROUP
    out_rows = planes * rows
    width = planes * (rows + 2 * HALO)
    devices = ngx * ngy
    gx = lax.axis_index("gx")
    gy = lax.axis_index("gy")
    me = gx * ngy + gy
    other = ngy - 1 - gy
    has_low = gx > 0
    has_high = gx < ngx - 1

    def peer(step):
        target = lax.rem(me + step, devices)
        return {"gx": lax.div(target, ngy), "gy": lax.rem(target, ngy)}

    barrier = pltpu.get_barrier_semaphore()

    def greet(step, carry):
        pl.semaphore_signal(barrier, inc=1, device_id=peer(step), device_id_type=MESH)
        return carry

    lax.fori_loop(1, devices, greet, 0)

    volume_copy = pltpu.make_async_copy(
        volume_ref, own.at[:, :, pl.ds(LANES, columns)], local_sem.at[0]
    )
    mask_copy = pltpu.make_async_copy(mask_ref, masked, local_sem.at[1])
    volume_copy.start()
    mask_copy.start()

    outside = pl.ds(pl.multiple_of(gy * (columns + LANES), LANES), LANES)
    own[:, :, outside] = jnp.zeros((planes, rows, LANES), jnp.float32)
    halo[:, :, :, outside] = jnp.zeros((2, planes, HALO, LANES), jnp.float32)

    @pl.when(jnp.logical_not(has_low))
    def _():
        halo[0] = jnp.zeros((planes, HALO, columns + 2 * LANES), jnp.float32)

    @pl.when(jnp.logical_not(has_high))
    def _():
        halo[1] = jnp.zeros((planes, HALO, columns + 2 * LANES), jnp.float32)

    def row_target(direction):
        return jnp.minimum(gx + 1, ngx - 1) if direction == 0 else jnp.maximum(gx - 1, 0)

    def rows_out(direction):
        return pl.ds(rows - HALO if direction == 0 else 0, HALO)

    edge_from = pl.ds(pl.multiple_of(other * (columns - LANES), LANES), LANES)
    edge_to = pl.ds(pl.multiple_of(gy * (columns + LANES), LANES), LANES)

    edge_copy = pltpu.make_async_remote_copy(
        src_ref=volume_ref.at[:, :, edge_from],
        dst_ref=own.at[:, :, edge_to],
        send_sem=edge_sem.at[0, 0],
        recv_sem=edge_sem.at[1, 0],
        device_id={"gy": other},
        device_id_type=MESH,
    )

    def corner_copy(direction):
        return pltpu.make_async_remote_copy(
            src_ref=volume_ref.at[:, rows_out(direction), edge_from],
            dst_ref=halo.at[direction, :, :, edge_to],
            send_sem=edge_sem.at[0, 1 + direction],
            recv_sem=edge_sem.at[1, 1 + direction],
            device_id={"gx": row_target(direction), "gy": other},
            device_id_type=MESH,
        )

    def halo_copy(direction, start, size, piece):
        return pltpu.make_async_remote_copy(
            src_ref=volume_ref.at[:, rows_out(direction), pl.ds(start, size)],
            dst_ref=halo.at[
                direction, :, :, pl.ds(pl.multiple_of(start + LANES, LANES), size)
            ],
            send_sem=halo_send.at[direction, piece],
            recv_sem=halo_recv.at[direction, piece],
            device_id={"gx": row_target(direction)},
            device_id_type=MESH,
        )

    def first_piece(direction):
        return halo_copy(direction, 0, LANES, 0)

    def middle_piece(direction, group):
        start = pl.multiple_of(group * GROUP + LANES, LANES)
        return halo_copy(direction, start, GROUP, group + 1)

    def last_piece(direction):
        return halo_copy(direction, columns - GROUP + LANES, GROUP - LANES, groups)

    sends_to = (has_high, has_low)
    gets_from = (has_low, has_high)

    build_matrices(index_ref, planes, rows, tmat, bmat)
    volume_copy.wait()
    mask_copy.wait()
    weights = masked[...].astype(jnp.float32)
    values = own[:, :, pl.ds(LANES, columns)]
    count = jnp.sum(weights)
    summed = jnp.sum(weights * values)
    deviation = values - summed / jnp.maximum(count, 1.0)
    squares = jnp.sum(weights * deviation * deviation)
    line = lax.broadcasted_iota(jnp.int32, (8, LANES), 0)
    mine[...] = jnp.where(line == 0, count, jnp.where(line == 1, summed, squares))

    pl.semaphore_wait(barrier, devices - 1)
    edge_copy.start()
    for direction in range(2):

        @pl.when(sends_to[direction])
        def _():
            corner_copy(direction).start()
            first_piece(direction).start()

    def send_middle(group, carry):
        for direction in range(2):

            @pl.when(sends_to[direction])
            def _():
                middle_piece(direction, group).start()

        return carry

    lax.fori_loop(0, groups - 1, send_middle, 0)
    for direction in range(2):

        @pl.when(sends_to[direction])
        def _():
            last_piece(direction).start()

    def stat_copy(step):
        return pltpu.make_async_remote_copy(
            src_ref=mine,
            dst_ref=others.at[step - 1],
            send_sem=stat_send.at[step - 1],
            recv_sem=stat_recv.at[step - 1],
            device_id=peer(step),
            device_id_type=MESH,
        )

    def send_stat(step, carry):
        stat_copy(step).start()
        return carry

    lax.fori_loop(1, devices, send_stat, 0)


    edge_copy.wait_recv()
    for direction in range(2):

        @pl.when(gets_from[direction])
        def _():
            corner_copy(direction).wait_recv()
            first_piece(direction).wait_recv()

    def out_copy(level, group):
        lanes = pl.ds(pl.multiple_of(group * GROUP, GROUP), GROUP)
        return pltpu.make_async_copy(
            result.at[level, :, :, lanes],
            raw_ref.at[level, :, :, lanes],
            out_sem.at[level, group],
        )

    def body(group, carry):
        for direction in range(2):

            @pl.when(jnp.logical_and(gets_from[direction], group < groups - 1))
            def _():
                middle_piece(direction, jnp.minimum(group, groups - 2)).wait_recv()

            @pl.when(jnp.logical_and(gets_from[direction], group == groups - 1))
            def _():
                last_piece(direction).wait_recv()

        start = pl.multiple_of(group * GROUP, GROUP)
        load = pl.ds(start, GROUP + 2 * LANES)
        block = jnp.concatenate(
            [
                own[:, :, load].reshape(out_rows, GROUP + 2 * LANES),
                halo[:, :, :, load].reshape(2 * planes * HALO, GROUP + 2 * LANES),
            ],
            axis=0,
        )[:, LANES - HALO : GROUP + 2 * LANES - HALO]
        high, low = split(block)
        left = jnp.concatenate(
            [
                jnp.concatenate([part[:, s : s + 2 * LANES] for part in (high, high, low)], axis=1)
                for s in range(0, GROUP, LANES)
            ],
            axis=0,
        )
        along_y = jnp.dot(left, tmat[...], preferred_element_type=jnp.float32)
        for level in range(2):
            kinds = [
                jnp.concatenate(
                    [
                        along_y[
                            s * width : (s + 1) * width,
                            (level * 3 + kind) * LANES : (level * 3 + kind + 1) * LANES,
                        ]
                        for s in range(GROUP // LANES)
                    ],
                    axis=1,
                )
                for kind in range(3)
            ]
            high, low = split(jnp.concatenate(kinds, axis=0))
            projected = jnp.dot(
                bmat[level],
                jnp.concatenate([high, high, low], axis=0),
                preferred_element_type=jnp.float32,
            )
            total = None
            for j in range(6):
                part = projected[j * out_rows : (j + 1) * out_rows]
                total = part * part if total is None else total + part * part
            result[level, :, :, pl.ds(start, GROUP)] = total.reshape(planes, rows, GROUP)
            out_copy(level, group).start()
        return carry

    lax.fori_loop(0, groups, body, 0)

    def wait_stat(step, carry):
        stat_copy(step).wait_recv()
        return carry

    lax.fori_loop(1, devices, wait_stat, 0)
    mine_now = mine[...]
    gathered = others[...]
    counts = gathered[:, 0, :]
    sums = gathered[:, 1, :]
    counted = mine_now[0:1] + jnp.sum(counts, axis=0, keepdims=True)
    centre = (mine_now[1:2] + jnp.sum(sums, axis=0, keepdims=True)) / counted
    apart = sums / jnp.maximum(counts, 1.0) - centre
    mine_apart = mine_now[1:2] / jnp.maximum(mine_now[0:1], 1.0) - centre
    spread = jnp.sum(gathered[:, 2, :] + counts * apart * apart, axis=0, keepdims=True) + (
        mine_now[2:3] + mine_now[0:1] * mine_apart * mine_apart
    )
    variance = spread / (counted - 1.0) + epsilon
    scale_ref[...] = jnp.broadcast_to(1.0 / (6.0 * variance), (8, LANES))

    edge_copy.wait_send()
    for direction in range(2):

        @pl.when(sends_to[direction])
        def _():
            corner_copy(direction).wait_send()
            first_piece(direction).wait_send()
            last_piece(direction).wait_send()

    def end_middle(group, carry):
        for direction in range(2):

            @pl.when(sends_to[direction])
            def _():
                middle_piece(direction, group).wait_send()

        return carry

    lax.fori_loop(0, groups - 1, end_middle, 0)

    def end_stat(step, carry):
        stat_copy(step).wait_send()
        return carry

    lax.fori_loop(1, devices, end_stat, 0)

    def end_out(group, carry):
        for level in range(2):
            out_copy(level, group).wait()
        return carry

    lax.fori_loop(0, groups, end_out, 0)


def scale_kernel(factor_ref, raw_ref, fine_ref, coarse_ref):
    factor = factor_ref[0:1, 0:1].reshape(1, 1, 1)
    fine_ref[...] = raw_ref[0] * factor
    coarse_ref[...] = raw_ref[1] * factor


def per_device(volume, mask, res_index):
    planes, rows, columns = volume.shape
    ngx = lax.axis_size("gx")
    ngy = lax.axis_size("gy")
    devices = ngx * ngy
    groups = columns // GROUP
    width = planes * (rows + 2 * HALO)
    extended = columns + 2 * LANES
    out = jax.ShapeDtypeStruct(volume.shape, jnp.float32)
    raw, factor = pl.pallas_call(
        functools.partial(kernel, ngx, ngy),
        out_shape=(
            jax.ShapeDtypeStruct((2,) + volume.shape, jnp.float32),
            jax.ShapeDtypeStruct((8, LANES), jnp.float32),
        ),
        in_specs=[
            pl.BlockSpec(memory_space=pltpu.SMEM),
            pl.BlockSpec(memory_space=pl.ANY),
            pl.BlockSpec(memory_space=pl.ANY),
        ],
        out_specs=(
            pl.BlockSpec(memory_space=pl.ANY),
            pl.BlockSpec(memory_space=pltpu.VMEM),
        ),
        scratch_shapes=[
            pltpu.VMEM((planes, rows, extended), jnp.float32),
            pltpu.VMEM((2, planes, HALO, extended), jnp.float32),
            pltpu.VMEM((planes, rows, columns), jnp.int32),
            pltpu.VMEM((6 * LANES, 6 * LANES), jnp.bfloat16),
            pltpu.VMEM((2, 6 * planes * rows, 9 * width), jnp.bfloat16),
            pltpu.VMEM((2, planes, rows, columns), jnp.float32),
            pltpu.VMEM((8, LANES), jnp.float32),
            pltpu.VMEM((devices - 1, 8, LANES), jnp.float32),
            pltpu.SemaphoreType.DMA((2,)),
            pltpu.SemaphoreType.DMA((2, 3)),
            pltpu.SemaphoreType.DMA((2, groups + 1)),
            pltpu.SemaphoreType.DMA((2, groups + 1)),
            pltpu.SemaphoreType.DMA((devices - 1,)),
            pltpu.SemaphoreType.DMA((devices - 1,)),
            pltpu.SemaphoreType.DMA((2, groups)),
        ],
        compiler_params=pltpu.CompilerParams(
            collective_id=0, has_side_effects=True, vmem_limit_bytes=60 * 1024 * 1024
        ),
        cost_estimate=pl.CostEstimate(
            flops=6_000_000_000, bytes_accessed=2_500_000, transcendentals=100_000
        ),
        name="resolution_statistic",
    )(res_index, volume, mask)

    block = pl.BlockSpec((planes, rows, columns // 2), lambda i: (0, 0, i))
    return pl.pallas_call(
        scale_kernel,
        grid=(2,),
        out_shape=(out, out),
        in_specs=[
            pl.BlockSpec((8, LANES), lambda i: (0, 0)),
            pl.BlockSpec((2, planes, rows, columns // 2), lambda i: (0, 0, 0, i)),
        ],
        out_specs=(block, block),
        name="scale_statistic",
    )(factor, raw)


def solution(mesh):
    placed = (P(None, ("parts", "gx"), "gy"), P(None, ("parts", "gx"), "gy"), P("parts"))
    return jax.shard_map(
        per_device,
        mesh=mesh,
        in_specs=placed,
        out_specs=(P(None, ("parts", "gx"), "gy"), P(None, ("parts", "gx"), "gy")),
        check_vma=False,
    )
```
